32 devices in a mesh: table: 16 (over z, y, x), score: 2 (over core).
Axes of the slice: x: 2, y: 2, z: 4, core: 2. Of those that a mesh axis runs over, the one named last changes fastest.
Arguments:
- hot_item_table: float32 [2048, 128], replicated, may hold values from -6 to 6
- cold_item_table: float32 [16384, 128], P('table'), may hold values from -6 to 6
- hist_rows: int32 [128, 512], P('table', 'score'), may hold values from 0 to 18431, as said below
- cand_rows: int32 [128, 512], P('table', 'score'), may hold values from 0 to 18431, as said below
- w_query: bfloat16 [128, 128], replicated, may hold values from -0.5 to 0.5
- w_key: bfloat16 [128, 128], replicated, may hold values from -0.5 to 0.5
- w_first: bfloat16 [256, 1024], replicated, may hold values from -0.5 to 0.5
- w_second: bfloat16 [1, 1024, 1024], replicated, may hold values from -0.25 to 0.25
- w_out: bfloat16 [1024], replicated, may hold values from -0.25 to 0.25
Outputs:
- scores: float32 [128, 512], P('table', 'score')
The draws below stay inside these ranges and needn't reach their ends.
Inputs may be any that keep to these rules, and one draw needn't show every extreme that they name: `hist_rows`: among the history items of one device (8 requests, 256 items each), at most 128 name cold rows of any one owner; for each index along score, one owner is named exactly 128 times by every device along table. `cand_rows`: among the candidates of one device (8 requests, 256 candidates each), at most 128 name cold rows of any one owner; for each index along score, one owner is named exactly 128 times by every device along table.
All inputs are finite; a program needn't handle non-finite values.
Results may differ from the reference program's by a relative error of at most 0.0072.
Values may be sent and summed in bfloat16 or wider, within the bound.
A program may use at most 64 MiB of HBM per device.

```python
import math
import jax
import jax.numpy as jnp
from jax import lax

E = 128
A = 128
FF = 1024
LAYERS = 1
H = 512
HOT = 2048
COLD_DEV = 1024
R_DEV = 8
C_DEV = 256
H_DEV = 256
CAP_H = 128
CAP_C = 128
N_TABLE = 16
N_SCORE = 2


def draw_codes(key, width_dev, slot_capacity):
    item_count = R_DEV * width_dev
    grid_shape = (N_TABLE, N_SCORE, item_count)
    subkeys = jax.random.split(key, 8)
    first_pick = jax.random.randint(subkeys[0], grid_shape, 0, N_TABLE)
    second_pick = jax.random.randint(subkeys[1], grid_shape, 0, N_TABLE)
    relabel = jax.random.permutation(subkeys[2], N_TABLE)
    owner_id = relabel[jnp.minimum(first_pick, second_pick)]
    cold_draw = jax.random.randint(subkeys[3], grid_shape, 0, 5) < 3
    heavy_owner = jax.random.randint(subkeys[4], (N_SCORE,), 0, N_TABLE)[None, :, None]
    ranking = jax.random.randint(subkeys[5], grid_shape, 0, 65536) * item_count + jnp.arange(item_count, dtype=jnp.int32)
    position = jnp.argsort(jnp.argsort(ranking, axis=-1), axis=-1)
    forced = position < slot_capacity
    owner_id = jnp.where(forced, heavy_owner, owner_id)
    cold_free = jnp.logical_and(cold_draw, jnp.logical_not(forced))
    owner_match = jnp.logical_and(owner_id[..., None] == jnp.arange(N_TABLE, dtype=jnp.int32), cold_free[..., None]).astype(jnp.int32)
    before = jnp.cumsum(owner_match, axis=2) - owner_match
    earlier = jnp.sum(before * owner_match, axis=-1)
    preloaded = jnp.where(owner_id == heavy_owner, slot_capacity, 0)
    kept_cold = jnp.logical_and(cold_free, earlier + preloaded < slot_capacity)
    is_cold = jnp.logical_or(forced, kept_cold)
    slot_id = jax.random.randint(subkeys[6], grid_shape, 0, COLD_DEV)
    hot_id = jax.random.randint(subkeys[7], grid_shape, 0, HOT)
    row_code = jnp.where(is_cold, HOT + owner_id * COLD_DEV + slot_id, hot_id).astype(jnp.int32)
    row_code = row_code.reshape(N_TABLE, N_SCORE, R_DEV, width_dev).transpose(0, 2, 1, 3)
    return row_code.reshape(N_TABLE * R_DEV, N_SCORE * width_dev)


def draw_hist_rows(key, part):
    return draw_codes(jax.random.fold_in(key, 11), H_DEV, CAP_H)


def draw_cand_rows(key, part):
    return draw_codes(jax.random.fold_in(key, 23), C_DEV, CAP_C)


def block_levels(stream_key, shape, shards, least, high):
    factor_of, own = 1.0, jax.random.fold_in(stream_key, 6)
    for axis_at, blocks in shards:
        steps = jnp.exp(jax.random.uniform(jax.random.fold_in(own, axis_at), (blocks,), jnp.float32, least / len(shards), high / len(shards)))
        factor_of = factor_of * jnp.repeat(steps, shape[axis_at] // blocks).reshape([-1 if axis == axis_at else 1 for axis in range(len(shape))])
    return factor_of


def normal_values(rng, shape, scale, limit, cuts=(), kind=jnp.bfloat16):
    result = jax.random.normal(rng, shape, jnp.float32) * scale
    if len(cuts) > 0:
        result = block_levels(rng, shape, cuts, -0.22, 0.18) * result
    return jnp.clip(result, min=-limit, max=limit).astype(kind)


def setup_inputs(seed: int = 0) -> dict:
    streams_of = jax.random.split(jax.random.key(seed), 10)
    hot_item_table = normal_values(streams_of[0], (HOT, E), 1.0, 6.0, (), jnp.float32)
    cold_item_table = normal_values(streams_of[1], (COLD_DEV * N_TABLE, E), 1.0, 6.0, ((0, 16),), jnp.float32)
    hist_rows = draw_hist_rows(jax.random.fold_in(streams_of[9], 71), 0)
    cand_rows = draw_cand_rows(jax.random.fold_in(streams_of[9], 71), 0)
    w_query = normal_values(streams_of[4], (E, A), E ** -0.5, 0.5)
    w_key = normal_values(streams_of[5], (E, A), E ** -0.5, 0.5)
    w_first = normal_values(streams_of[6], (2 * E, FF), E ** -0.5, 0.5)
    w_second = normal_values(streams_of[7], (LAYERS, FF, FF), (FF // 2) ** -0.5, 0.25)
    w_out = normal_values(streams_of[8], (FF,), (FF // 2) ** -0.5, 0.25)
    return {"hot_item_table": hot_item_table, "cold_item_table": cold_item_table, "hist_rows": hist_rows, "cand_rows": cand_rows, "w_query": w_query, "w_key": w_key, "w_first": w_first, "w_second": w_second, "w_out": w_out}


def reference(hot_item_table, cold_item_table, hist_rows, cand_rows, w_query, w_key, w_first, w_second, w_out):
    full_table = jnp.concatenate([hot_item_table, cold_item_table], axis=0)
    score_scale = 1.0 / math.sqrt(A)
    pool_scale = 1.0 / math.sqrt(H)

    def one_request(request_codes):
        history_codes, candidate_codes = request_codes
        history_bf = jnp.take(full_table, history_codes.astype(jnp.int32), axis=0).astype(jnp.bfloat16)
        candidate_bf = jnp.take(full_table, candidate_codes.astype(jnp.int32), axis=0).astype(jnp.bfloat16)
        queries = jnp.dot(candidate_bf, w_query, preferred_element_type=jnp.float32).astype(jnp.bfloat16)
        key_rows = jnp.dot(history_bf, w_key, preferred_element_type=jnp.float32).astype(jnp.bfloat16)
        logits = jnp.dot(queries, key_rows.T, preferred_element_type=jnp.float32) * score_scale
        attend = jax.nn.sigmoid(logits).astype(jnp.bfloat16)
        pooled = (jnp.dot(attend, history_bf, preferred_element_type=jnp.float32) * pool_scale).astype(jnp.bfloat16)
        joined = jnp.concatenate([candidate_bf, pooled], axis=1)
        hidden = jnp.maximum(jnp.dot(joined, w_first, preferred_element_type=jnp.float32), 0.0).astype(jnp.bfloat16)
        for layer_idx in range(LAYERS):
            hidden = jnp.maximum(jnp.dot(hidden, w_second[layer_idx], preferred_element_type=jnp.float32), 0.0).astype(jnp.bfloat16)
        return jnp.dot(hidden, w_out, preferred_element_type=jnp.float32)
    return lax.map(one_request, (hist_rows, cand_rows))
```

```python
import math

import jax
import jax.numpy as jnp
from jax import lax
from jax.sharding import PartitionSpec as P

H = 512
HOT = 2048
COLD_DEV = 1024


def owner_positions(owner_match):
    item_total, owner_count = owner_match.shape
    block = math.gcd(item_total, 128)
    blocks = item_total // block
    match_bf = owner_match.astype(jnp.bfloat16).reshape(blocks, block, owner_count)
    lower = (
        lax.broadcasted_iota(jnp.int32, (block, block), 0)
        > lax.broadcasted_iota(jnp.int32, (block, block), 1)
    ).astype(jnp.bfloat16)
    within = jnp.einsum("ij,kjo->kio", lower, match_bf, preferred_element_type=jnp.float32)
    totals = jnp.sum(match_bf.astype(jnp.float32), axis=1)
    earlier = (
        lax.broadcasted_iota(jnp.int32, (blocks, blocks), 0)
        > lax.broadcasted_iota(jnp.int32, (blocks, blocks), 1)
    ).astype(jnp.float32)
    offsets = jnp.einsum(
        "bk,ko->bo", earlier, totals, precision=lax.Precision.HIGHEST, preferred_element_type=jnp.float32
    )
    before = (within + offsets[:, None, :]).reshape(item_total, owner_count)
    return jnp.sum(before * owner_match, axis=1).astype(jnp.int32)


def gather_owner_rows(
    grouped_item_codes, owner_capacity_list, hot_item_table, cold_item_table, table_row_count
):
    owner_iota = jnp.arange(table_row_count, dtype=jnp.int32)
    layouts = []
    outgoing = []
    for item_row_codes, slot_capacity in zip(grouped_item_codes, owner_capacity_list):
        is_cold = item_row_codes >= HOT
        relative = jnp.where(is_cold, item_row_codes - HOT, 0)
        owner_id = relative // COLD_DEV
        slot_id = relative % COLD_DEV
        owner_match = jnp.logical_and(
            owner_id[:, None] == owner_iota[None, :], is_cold[:, None]
        ).astype(jnp.float32)
        position = owner_positions(owner_match)
        flat_index = owner_id * slot_capacity + position
        slot_onehot = (
            position[:, None] == jnp.arange(slot_capacity, dtype=jnp.int32)[None, :]
        ).astype(jnp.float32)
        weighted = owner_match * slot_id.astype(jnp.float32)[:, None]
        requests_out = jnp.einsum(
            "io,is->os",
            weighted,
            slot_onehot,
            precision=lax.Precision.HIGHEST,
            preferred_element_type=jnp.float32,
        )
        outgoing.append(requests_out.astype(jnp.int32))
        layouts.append((item_row_codes, is_cold, flat_index, slot_capacity))
    wanted_all = jnp.concatenate(outgoing, axis=1)
    cold_rows = jnp.take(
        cold_item_table,
        lax.all_to_all(wanted_all, "table", split_axis=0, concat_axis=0, tiled=True),
        axis=0,
    ).astype(jnp.bfloat16)
    fetched = lax.all_to_all(cold_rows, "table", split_axis=0, concat_axis=0, tiled=True)
    results = []
    column_start = 0
    for item_row_codes, is_cold, flat_index, slot_capacity in layouts:
        flat_rows = fetched[:, column_start : column_start + slot_capacity].reshape(
            table_row_count * slot_capacity, fetched.shape[2]
        )
        picked = jnp.take(flat_rows, jnp.where(is_cold, flat_index, 0), axis=0)
        hot_rows = jnp.take(hot_item_table, jnp.where(is_cold, 0, item_row_codes), axis=0).astype(
            jnp.bfloat16
        )
        results.append(jnp.where(is_cold[:, None], picked, hot_rows))
        column_start = column_start + slot_capacity
    return results


def body(
    hot_item_table, cold_item_table, hist_rows, cand_rows, w_query, w_key, w_first, w_second, w_out
):
    table_row_count = lax.axis_size("table")
    requests, h_dev = hist_rows.shape
    c_dev = cand_rows.shape[1]
    width = hot_item_table.shape[1]
    cap_h = max(2, requests * h_dev // table_row_count)
    cap_c = max(2, requests * c_dev // table_row_count)
    history_emb, candidate_emb = gather_owner_rows(
        [hist_rows.reshape(-1), cand_rows.reshape(-1)],
        [cap_h, cap_c],
        hot_item_table,
        cold_item_table,
        table_row_count,
    )
    candidate_bf = candidate_emb.reshape(requests, c_dev, width)
    queries = jnp.einsum(
        "rce,ea->rca", candidate_bf, w_query, preferred_element_type=jnp.float32
    ).astype(jnp.bfloat16)
    score_scale = 1.0 / math.sqrt(w_query.shape[1])
    history_bf = history_emb.reshape(requests, h_dev, width)
    shard_rows = lax.all_gather(history_bf, "score", axis=1, tiled=True)
    key_rows = jnp.einsum(
        "rhe,ea->rha", shard_rows, w_key, preferred_element_type=jnp.float32
    ).astype(jnp.bfloat16)
    logits = (
        jnp.einsum("rca,rha->rch", queries, key_rows, preferred_element_type=jnp.float32)
        * score_scale
    )
    weights = jax.nn.sigmoid(logits).astype(jnp.bfloat16)
    pooled_sum = jnp.einsum("rch,rhe->rce", weights, shard_rows, preferred_element_type=jnp.float32)
    pooled = (pooled_sum * (1.0 / math.sqrt(H))).astype(jnp.bfloat16)
    joined = jnp.concatenate([candidate_bf, pooled], axis=2).reshape(requests * c_dev, 2 * width)
    hidden = jnp.maximum(jnp.dot(joined, w_first, preferred_element_type=jnp.float32), 0.0).astype(
        jnp.bfloat16
    )
    hidden = jnp.maximum(
        jnp.dot(hidden, w_second[0], preferred_element_type=jnp.float32), 0.0
    ).astype(jnp.bfloat16)
    ranked = jnp.dot(hidden, w_out, preferred_element_type=jnp.float32)
    return ranked.reshape(requests, c_dev)


def solution(mesh):
    return jax.shard_map(
        body,
        mesh=mesh,
        in_specs=(
            P(),
            P("table", None),
            P("table", "score"),
            P("table", "score"),
            P(),
            P(),
            P(),
            P(),
            P(),
        ),
        out_specs=P("table", "score"),
        check_vma=False,
    )
```

```python
import math

import jax
import jax.numpy as jnp
from jax import lax
from jax.experimental import pallas as pl
from jax.experimental.pallas import tpu as pltpu
from jax.sharding import PartitionSpec as P

UNROLL = 32
GROUP = 2


def score_kernel(
    hist_ref,
    cand_ref,
    hot_ref,
    cold_ref,
    w_query_ref,
    w_key_ref,
    w_first_ref,
    w_second_ref,
    w_out_ref,
    out_ref,
    table,
    history,
    candidates,
):
    shards, requests, h_dev = hist_ref.shape
    c_dev = cand_ref.shape[1]
    hot_rows, width = hot_ref.shape
    h_total = shards * h_dev
    score_scale = 1.0 / math.sqrt(w_query_ref.shape[1])
    pool_scale = 1.0 / math.sqrt(h_total)

    table[pl.ds(0, hot_rows), :] = hot_ref[...]
    step = 512

    @pl.loop(0, cold_ref.shape[0] // step)
    def _(i):
        at = pl.multiple_of(i * step, step)
        to = pl.multiple_of(hot_rows + i * step, step)
        table[pl.ds(to, step), :] = cold_ref[pl.ds(at, step), :].astype(jnp.float32)

    @pl.loop(0, requests)
    def _(r):
        for s in range(shards):

            @pl.loop(0, h_dev // UNROLL)
            def _(block):
                base = pl.multiple_of(block * UNROLL, UNROLL)
                for u in range(UNROLL):
                    row = hist_ref[s, r, base + u]
                    history[r, pl.ds(s * h_dev + base + u, 1), :] = table[pl.ds(row, 1), :]

        @pl.loop(0, c_dev // UNROLL)
        def _(block):
            base = pl.multiple_of(block * UNROLL, UNROLL)
            for u in range(UNROLL):
                row = cand_ref[r, base + u]
                candidates[r, pl.ds(base + u, 1), :] = table[pl.ds(row, 1), :]

    w_out = jnp.broadcast_to(w_out_ref[...], (16, w_out_ref.shape[1]))

    @pl.loop(0, requests // GROUP)
    def _(g):
        joined = []
        for q in range(GROUP):
            r = g * GROUP + q
            hist = history[r].astype(jnp.bfloat16)
            cand = candidates[r].astype(jnp.bfloat16)
            query = jnp.dot(cand, w_query_ref[...], preferred_element_type=jnp.float32).astype(
                jnp.bfloat16
            )
            key = jnp.dot(hist, w_key_ref[...], preferred_element_type=jnp.float32).astype(
                jnp.bfloat16
            )
            logits = lax.dot_general(
                query, key, (((1,), (1,)), ((), ())), preferred_element_type=jnp.float32
            )
            attend = jax.nn.sigmoid(logits * score_scale).astype(jnp.bfloat16)
            pooled = jnp.dot(attend, hist, preferred_element_type=jnp.float32) * pool_scale
            joined.append(jnp.concatenate([cand, pooled.astype(jnp.bfloat16)], axis=1))
        joined = jnp.concatenate(joined, axis=0)
        first = jnp.dot(joined, w_first_ref[...], preferred_element_type=jnp.float32)
        first = jnp.maximum(first, 0.0).astype(jnp.bfloat16)
        deep = jnp.dot(first, w_second_ref[...], preferred_element_type=jnp.float32)
        deep = jnp.maximum(deep, 0.0).astype(jnp.bfloat16)
        ranked = lax.dot_general(
            w_out, deep, (((1,), (1,)), ((), ())), preferred_element_type=jnp.float32
        )
        for q in range(GROUP):
            out_ref[pl.ds(g * GROUP + q, 1), :] = ranked[0:1, q * c_dev : (q + 1) * c_dev]


def body(
    hot_item_table, cold_item_table, hist_rows, cand_rows, w_query, w_key, w_first, w_second, w_out
):
    requests, h_dev = hist_rows.shape
    c_dev = cand_rows.shape[1]
    hot_rows, width = hot_item_table.shape
    cold_all = lax.all_gather(cold_item_table.astype(jnp.bfloat16), "table", axis=0, tiled=True)
    hist_all = lax.all_gather(hist_rows, "score", axis=0)
    shards = hist_all.shape[0]
    vmem = pl.BlockSpec(memory_space=pltpu.VMEM)
    smem = pl.BlockSpec(memory_space=pltpu.SMEM)
    return pl.pallas_call(
        score_kernel,
        out_shape=jax.ShapeDtypeStruct((requests, c_dev), jnp.float32),
        in_specs=[smem, smem] + [vmem] * 7,
        out_specs=vmem,
        scratch_shapes=[
            pltpu.VMEM((hot_rows + cold_all.shape[0], width), jnp.float32),
            pltpu.VMEM((requests, shards * h_dev, width), jnp.float32),
            pltpu.VMEM((requests, c_dev, width), jnp.float32),
        ],
        compiler_params=pltpu.CompilerParams(vmem_limit_bytes=56 * 2**20),
        name="score_candidates",
    )(
        hist_all,
        cand_rows,
        hot_item_table,
        cold_all,
        w_query,
        w_key,
        w_first,
        w_second[0],
        w_out[None, :],
    )


def solution(mesh):
    return jax.shard_map(
        body,
        mesh=mesh,
        in_specs=(
            P(),
            P("table", None),
            P("table", "score"),
            P("table", "score"),
            P(),
            P(),
            P(),
            P(),
            P(),
        ),
        out_specs=P("table", "score"),
        check_vma=False,
    )
```

```python
import functools
import math

import jax
import jax.numpy as jnp
from jax import lax
from jax.experimental import pallas as pl
from jax.experimental.pallas import tpu as pltpu
from jax.sharding import PartitionSpec as P

UNROLL = 32
GROUP = 2


def score_kernel(
    hist_ref,
    cand_ref,
    hot_ref,
    cold_ref,
    w_query_ref,
    w_key_ref,
    w_first_ref,
    w_second_ref,
    w_out_ref,
    out_ref,
    table,
    history,
    candidates,
):
    shards, requests, h_dev = hist_ref.shape
    c_dev = cand_ref.shape[1]
    hot_rows, width = hot_ref.shape
    h_total = shards * h_dev
    score_scale = 1.0 / math.sqrt(w_query_ref.shape[1])
    pool_scale = 1.0 / math.sqrt(h_total)

    table[pl.ds(0, hot_rows), :] = hot_ref[...]
    step = 512

    @pl.loop(0, cold_ref.shape[0] // step)
    def _(i):
        at = pl.multiple_of(i * step, step)
        to = pl.multiple_of(hot_rows + i * step, step)
        table[pl.ds(to, step), :] = cold_ref[pl.ds(at, step), :].astype(jnp.float32)

    @pl.loop(0, requests)
    def _(r):
        for s in range(shards):

            @pl.loop(0, h_dev // UNROLL)
            def _(block):
                base = pl.multiple_of(block * UNROLL, UNROLL)
                for u in range(UNROLL):
                    row = hist_ref[s, r, base + u]
                    history[r, pl.ds(s * h_dev + base + u, 1), :] = table[pl.ds(row, 1), :]

        @pl.loop(0, c_dev // UNROLL)
        def _(block):
            base = pl.multiple_of(block * UNROLL, UNROLL)
            for u in range(UNROLL):
                row = cand_ref[r, base + u]
                candidates[r, pl.ds(base + u, 1), :] = table[pl.ds(row, 1), :]

    w_out = jnp.broadcast_to(w_out_ref[...], (16, w_out_ref.shape[1]))

    @pl.loop(0, requests // GROUP)
    def _(g):
        joined = []
        for q in range(GROUP):
            r = g * GROUP + q
            hist = history[r].astype(jnp.bfloat16)
            cand = candidates[r].astype(jnp.bfloat16)
            query = jnp.dot(cand, w_query_ref[...], preferred_element_type=jnp.float32).astype(
                jnp.bfloat16
            )
            key = jnp.dot(hist, w_key_ref[...], preferred_element_type=jnp.float32).astype(
                jnp.bfloat16
            )
            logits = lax.dot_general(
                query, key, (((1,), (1,)), ((), ())), preferred_element_type=jnp.float32
            )
            attend = jax.nn.sigmoid(logits * score_scale).astype(jnp.bfloat16)
            pooled = jnp.dot(attend, hist, preferred_element_type=jnp.float32) * pool_scale
            joined.append(jnp.concatenate([cand, pooled.astype(jnp.bfloat16)], axis=1))
        joined = jnp.concatenate(joined, axis=0)
        first = jnp.dot(joined, w_first_ref[...], preferred_element_type=jnp.float32)
        first = jnp.maximum(first, 0.0).astype(jnp.bfloat16)
        deep = jnp.dot(first, w_second_ref[...], preferred_element_type=jnp.float32)
        deep = jnp.maximum(deep, 0.0).astype(jnp.bfloat16)
        ranked = lax.dot_general(
            w_out, deep, (((1,), (1,)), ((), ())), preferred_element_type=jnp.float32
        )
        for q in range(GROUP):
            out_ref[pl.ds(g * GROUP + q, 1), :] = ranked[0:1, q * c_dev : (q + 1) * c_dev]


MESH = pl.DeviceIdType.MESH


def spread_kernel(
    n_table,
    n_score,
    cold_ref,
    hist_ref,
    out_ref,
    hist_out,
    own,
    recv_main,
    recv_diag,
    recv_peer,
    send_up,
    send_down,
    send_x,
    send_y,
    send_half_x,
    send_half_y,
    send_peer,
    hist_send,
    hist_recv,
    local_sem,
):
    depth = n_table // 4
    me = lax.axis_index("table")
    c = lax.axis_index("score")
    z, y, x = me // 4, (me // 2) % 2, me % 2
    rows = own.shape[1]
    half = rows // 2

    def at(zz, yy, xx):
        return (zz * 2 + yy) * 2 + xx

    def device(owner):
        return {"table": owner, "score": c}

    to_x, to_y = device(at(z, y, 1 - x)), device(at(z, 1 - y, x))
    to_up, to_down = device(at(z + 1, y, x)), device(at(z - 1, y, x))
    has_up, has_down = z < depth - 1, z > 0
    peers = [{"table": me, "score": (c + k) % n_score} for k in range(1, n_score)]

    barrier = pltpu.get_barrier_semaphore()
    for target in [to_x, to_y] + peers:
        pl.semaphore_signal(barrier, inc=1, device_id=target, device_id_type=MESH)
    for cond, target in ((has_up, to_up), (has_down, to_down)):

        @pl.when(cond)
        def _():
            pl.semaphore_signal(barrier, inc=1, device_id=target, device_id_type=MESH)

    for s in range(n_score):
        own[s] = cold_ref[pl.ds(s * rows, rows), :].astype(jnp.bfloat16)

    along_z = has_up.astype(jnp.int32) + has_down.astype(jnp.int32)
    pl.semaphore_wait(barrier, 2 + len(peers) + along_z)

    def copy(src, dst, send, recv, target):
        return pltpu.make_async_remote_copy(
            src_ref=src,
            dst_ref=dst,
            send_sem=send,
            recv_sem=recv,
            device_id=target,
            device_id_type=MESH,
        )

    def whole(owner, send, target, src=None):
        src = out_ref.at[owner, c] if src is None else src
        return copy(src, out_ref.at[owner, c], send, recv_main.at[owner], target)

    def part(owner, zz, which, send, target):
        block = out_ref.at[owner, c, pl.ds(which * half, half)]
        return copy(block, block, send, recv_diag.at[zz, which], target)

    def to_peers(owner):
        return [
            copy(
                out_ref.at[owner, c],
                out_ref.at[owner, c],
                send_peer.at[owner, k],
                recv_peer.at[owner, c],
                target,
            )
            for k, target in enumerate(peers)
        ]

    def start(copies):
        for one in copies:
            one.start()

    def column(zz, src=None):
        owner = at(zz, y, x)
        return [whole(owner, send_x.at[zz], to_x, src), whole(owner, send_y.at[zz], to_y, src)]

    def upward(zz, src=None):
        return whole(at(zz, y, x), send_up.at[zz], to_up, src)

    def downward(zz, src=None):
        return whole(at(zz, y, x), send_down.at[zz], to_down, src)

    mine = own.at[c]

    @pl.when(has_up)
    def _():
        upward(z, mine).start()

    @pl.when(has_down)
    def _():
        downward(z, mine).start()

    start(column(z, mine))
    hist_copies = [
        copy(hist_ref, hist_out.at[c], hist_send.at[k], hist_recv.at[c], target)
        for k, target in enumerate(peers)
    ]
    start(hist_copies)
    local = [
        pltpu.make_async_copy(own, out_ref.at[me], local_sem.at[0]),
        pltpu.make_async_copy(hist_ref, hist_out.at[c], local_sem.at[1]),
    ]
    start(local)

    def sides(d):
        if d == 0:
            return [(z, None)]
        return [(z - d, z - d >= 0), (z + d, z + d < depth)]

    def guarded(cond, run):
        if cond is None:
            run()
        else:
            pl.when(cond)(run)

    def from_column(d):
        for zz, cond in sides(d):

            def run(zz=zz):
                owner = at(zz, y, x)
                whole(owner, send_x.at[zz], to_x).wait_recv()

                @pl.when(jnp.logical_and(zz < z, has_up))
                def _():
                    upward(zz).start()

                @pl.when(jnp.logical_and(zz > z, has_down))
                def _():
                    downward(zz).start()

                start(column(zz))
                start(to_peers(owner))

            guarded(cond, run)

    def from_sides(d):
        for zz, cond in sides(d):

            def run(zz=zz):
                owner = at(zz, y, 1 - x)
                whole(owner, send_x.at[zz], to_x).wait_recv()
                part(owner, zz, 0, send_half_y.at[zz], to_y).start()
                start(to_peers(owner))
                owner = at(zz, 1 - y, x)
                whole(owner, send_x.at[zz], to_x).wait_recv()
                part(owner, zz, 1, send_half_x.at[zz], to_x).start()
                start(to_peers(owner))

            guarded(cond, run)

    def from_diagonal(d):
        for zz, cond in sides(d):

            def run(zz=zz):
                owner = at(zz, 1 - y, 1 - x)
                part(owner, zz, 0, send_half_y.at[zz], to_y).wait_recv()
                part(owner, zz, 1, send_half_x.at[zz], to_x).wait_recv()
                start(to_peers(owner))

            guarded(cond, run)

    for d in range(1, depth + 2):
        if d < depth:
            from_column(d)
        if d - 1 < depth:
            from_sides(d - 1)
        if 0 <= d - 2:
            from_diagonal(d - 2)

    def finish(zz, src=None):
        for one in column(zz, src):
            one.wait_send()
        part(at(zz, y, 1 - x), zz, 0, send_half_y.at[zz], to_y).wait_send()
        part(at(zz, 1 - y, x), zz, 1, send_half_x.at[zz], to_x).wait_send()

        @pl.when(jnp.logical_and(zz <= z, has_up))
        def _():
            upward(zz, src).wait_send()

        @pl.when(jnp.logical_and(zz >= z, has_down))
        def _():
            downward(zz, src).wait_send()

    for one in hist_copies:
        one.wait_send()
    for one in local:
        one.wait()
    for k in range(1, n_score):
        other = (c + k) % n_score
        copy(hist_ref, hist_out.at[other], hist_send.at[0], hist_recv.at[other], to_x).wait_recv()
    for zz in range(depth):
        finish(zz)
        for yy in range(2):
            for xx in range(2):
                owner = at(zz, yy, xx)

                @pl.when(owner != me)
                def _():
                    for one in to_peers(owner):
                        one.wait_send()
                    for k in range(1, n_score):
                        other = (c + k) % n_score
                        block = out_ref.at[owner, other]
                        copy(
                            block, block, send_peer.at[0, 0], recv_peer.at[owner, other], to_x
                        ).wait_recv()


def spread(cold_item_table, hist_rows):
    n_table, n_score = lax.axis_size("table"), lax.axis_size("score")
    cold_rows, width = cold_item_table.shape
    depth, rows = n_table // 4, cold_rows // n_score
    dma = pltpu.SemaphoreType.DMA
    anywhere = pl.BlockSpec(memory_space=pl.ANY)
    cold_all, hist_all = pl.pallas_call(
        functools.partial(spread_kernel, n_table, n_score),
        out_shape=(
            jax.ShapeDtypeStruct((n_table, n_score, rows, width), jnp.bfloat16),
            jax.ShapeDtypeStruct((n_score,) + hist_rows.shape, jnp.int32),
        ),
        in_specs=[pl.BlockSpec(memory_space=pltpu.VMEM)] * 2,
        out_specs=(anywhere, anywhere),
        scratch_shapes=[
            pltpu.VMEM((n_score, rows, width), jnp.bfloat16),
            dma((n_table,)),
            dma((depth, 2)),
            dma((n_table, n_score)),
            dma((depth,)),
            dma((depth,)),
            dma((depth,)),
            dma((depth,)),
            dma((depth,)),
            dma((depth,)),
            dma((n_table, n_score - 1)),
            dma((n_score - 1,)),
            dma((n_score,)),
            dma((2,)),
        ],
        compiler_params=pltpu.CompilerParams(
            collective_id=0, has_side_effects=True, vmem_limit_bytes=8 * 2**20
        ),
        name="spread_cold_rows",
    )(cold_item_table, hist_rows)
    return cold_all.reshape(n_table * cold_rows, width), hist_all


def body(
    hot_item_table, cold_item_table, hist_rows, cand_rows, w_query, w_key, w_first, w_second, w_out
):
    requests, h_dev = hist_rows.shape
    c_dev = cand_rows.shape[1]
    hot_rows, width = hot_item_table.shape
    cold_all, hist_all = spread(cold_item_table, hist_rows)
    shards = hist_all.shape[0]
    vmem = pl.BlockSpec(memory_space=pltpu.VMEM)
    smem = pl.BlockSpec(memory_space=pltpu.SMEM)
    return pl.pallas_call(
        score_kernel,
        out_shape=jax.ShapeDtypeStruct((requests, c_dev), jnp.float32),
        in_specs=[smem, smem] + [vmem] * 7,
        out_specs=vmem,
        scratch_shapes=[
            pltpu.VMEM((hot_rows + cold_all.shape[0], width), jnp.float32),
            pltpu.VMEM((requests, shards * h_dev, width), jnp.float32),
            pltpu.VMEM((requests, c_dev, width), jnp.float32),
        ],
        compiler_params=pltpu.CompilerParams(vmem_limit_bytes=56 * 2**20),
        name="score_candidates",
    )(
        hist_all,
        cand_rows,
        hot_item_table,
        cold_all,
        w_query,
        w_key,
        w_first,
        w_second[0],
        w_out[None, :],
    )


def solution(mesh):
    return jax.shard_map(
        body,
        mesh=mesh,
        in_specs=(
            P(),
            P("table", None),
            P("table", "score"),
            P("table", "score"),
            P(),
            P(),
            P(),
            P(),
            P(),
        ),
        out_specs=P("table", "score"),
        check_vma=False,
    )
```

```python
import functools
import math

import jax
import jax.numpy as jnp
from jax import lax
from jax.experimental import pallas as pl
from jax.experimental.pallas import tpu as pltpu
from jax.sharding import PartitionSpec as P

UNROLL = 32
GROUP = 2


def score_kernel(
    hist_ref,
    cand_ref,
    hot_ref,
    cold_ref,
    w_query_ref,
    w_key_ref,
    w_first_ref,
    w_second_ref,
    w_out_ref,
    out_ref,
    table,
    history,
    candidates,
):
    shards, requests, h_dev = hist_ref.shape
    c_dev = cand_ref.shape[1]
    hot_rows, width = hot_ref.shape
    h_total = shards * h_dev
    score_scale = 1.0 / math.sqrt(w_query_ref.shape[1])
    pool_scale = 1.0 / math.sqrt(h_total)

    table[pl.ds(0, hot_rows), :] = hot_ref[...]
    step = 512

    @pl.loop(0, cold_ref.shape[0] // step)
    def _(i):
        at = pl.multiple_of(i * step, step)
        to = pl.multiple_of(hot_rows + i * step, step)
        table[pl.ds(to, step), :] = cold_ref[pl.ds(at, step), :].astype(jnp.float32)

    @pl.loop(0, requests)
    def _(r):
        for s in range(shards):
            for start in range(0, h_dev, UNROLL):
                rows = [hist_ref[s, r, start + u] for u in range(UNROLL)]
                got = [table[pl.ds(row, 1), :] for row in rows]
                for u in range(UNROLL):
                    history[r, pl.ds(s * h_dev + start + u, 1), :] = got[u]
        for start in range(0, c_dev, UNROLL):
            rows = [cand_ref[r, start + u] for u in range(UNROLL)]
            got = [table[pl.ds(row, 1), :] for row in rows]
            for u in range(UNROLL):
                candidates[r, pl.ds(start + u, 1), :] = got[u]

    w_out = jnp.broadcast_to(w_out_ref[...][None, :], (16, w_out_ref.shape[0]))

    @pl.loop(0, requests // GROUP)
    def _(g):
        joined = []
        for q in range(GROUP):
            r = g * GROUP + q
            hist = history[r].astype(jnp.bfloat16)
            cand = candidates[r].astype(jnp.bfloat16)
            query = jnp.dot(cand, w_query_ref[...], preferred_element_type=jnp.float32).astype(
                jnp.bfloat16
            )
            key = jnp.dot(hist, w_key_ref[...], preferred_element_type=jnp.float32).astype(
                jnp.bfloat16
            )
            logits = lax.dot_general(
                query, key, (((1,), (1,)), ((), ())), preferred_element_type=jnp.float32
            )
            attend = (jnp.tanh(logits * (0.5 * score_scale)) * 0.5 + 0.5).astype(jnp.bfloat16)
            pooled = jnp.dot(attend, hist, preferred_element_type=jnp.float32) * pool_scale
            joined.append(jnp.concatenate([cand, pooled.astype(jnp.bfloat16)], axis=1))
        joined = jnp.concatenate(joined, axis=0)
        first = jnp.dot(joined, w_first_ref[...], preferred_element_type=jnp.float32)
        first = jnp.maximum(first, 0.0).astype(jnp.bfloat16)
        deep = jnp.dot(first, w_second_ref[...], preferred_element_type=jnp.float32)
        deep = jnp.maximum(deep, 0.0).astype(jnp.bfloat16)
        ranked = lax.dot_general(
            w_out, deep, (((1,), (1,)), ((), ())), preferred_element_type=jnp.float32
        )
        for q in range(GROUP):
            out_ref[pl.ds(g * GROUP + q, 1), :] = ranked[0:1, q * c_dev : (q + 1) * c_dev]


MESH = pl.DeviceIdType.MESH


def spread_kernel(
    n_table,
    n_score,
    cold_ref,
    hist_ref,
    out_ref,
    hist_out,
    own,
    recv_main,
    recv_diag,
    recv_peer,
    send_up,
    send_down,
    send_x,
    send_y,
    send_half_x,
    send_half_y,
    send_peer,
    hist_send,
    hist_recv,
    local_sem,
):
    depth = n_table // 4
    me = lax.axis_index("table")
    c = lax.axis_index("score")
    z, y, x = me // 4, (me // 2) % 2, me % 2
    rows = own.shape[1]
    half = rows // 2

    def at(zz, yy, xx):
        return (zz * 2 + yy) * 2 + xx

    def device(owner):
        return {"table": owner, "score": c}

    to_x, to_y = device(at(z, y, 1 - x)), device(at(z, 1 - y, x))
    to_up, to_down = device(at(z + 1, y, x)), device(at(z - 1, y, x))
    has_up, has_down = z < depth - 1, z > 0
    peers = [{"table": me, "score": (c + k) % n_score} for k in range(1, n_score)]

    barrier = pltpu.get_barrier_semaphore()
    for target in [to_x, to_y] + peers:
        pl.semaphore_signal(barrier, inc=1, device_id=target, device_id_type=MESH)
    for cond, target in ((has_up, to_up), (has_down, to_down)):

        @pl.when(cond)
        def _():
            pl.semaphore_signal(barrier, inc=1, device_id=target, device_id_type=MESH)

    for s in range(n_score):
        own[s] = cold_ref[pl.ds(s * rows, rows), :].astype(jnp.bfloat16)

    along_z = has_up.astype(jnp.int32) + has_down.astype(jnp.int32)
    pl.semaphore_wait(barrier, 2 + len(peers) + along_z)

    def copy(src, dst, send, recv, target):
        return pltpu.make_async_remote_copy(
            src_ref=src,
            dst_ref=dst,
            send_sem=send,
            recv_sem=recv,
            device_id=target,
            device_id_type=MESH,
        )

    def whole(owner, send, target, src=None):
        src = out_ref.at[owner, c] if src is None else src
        return copy(src, out_ref.at[owner, c], send, recv_main.at[owner], target)

    def part(owner, zz, which, send, target):
        block = out_ref.at[owner, c, pl.ds(which * half, half)]
        return copy(block, block, send, recv_diag.at[zz, which], target)

    def to_peers(owner):
        return [
            copy(
                out_ref.at[owner, c],
                out_ref.at[owner, c],
                send_peer.at[owner, k],
                recv_peer.at[owner, c],
                target,
            )
            for k, target in enumerate(peers)
        ]

    def start(copies):
        for one in copies:
            one.start()

    def column(zz, src=None):
        owner = at(zz, y, x)
        return [whole(owner, send_x.at[zz], to_x, src), whole(owner, send_y.at[zz], to_y, src)]

    def upward(zz, src=None):
        return whole(at(zz, y, x), send_up.at[zz], to_up, src)

    def downward(zz, src=None):
        return whole(at(zz, y, x), send_down.at[zz], to_down, src)

    mine = own.at[c]

    @pl.when(has_up)
    def _():
        upward(z, mine).start()

    @pl.when(has_down)
    def _():
        downward(z, mine).start()

    start(column(z, mine))
    hist_copies = [
        copy(hist_ref, hist_out.at[c], hist_send.at[k], hist_recv.at[c], target)
        for k, target in enumerate(peers)
    ]
    start(hist_copies)
    local = [
        pltpu.make_async_copy(own, out_ref.at[me], local_sem.at[0]),
        pltpu.make_async_copy(hist_ref, hist_out.at[c], local_sem.at[1]),
    ]
    start(local)

    def sides(d):
        if d == 0:
            return [(z, None)]
        return [(z - d, z - d >= 0), (z + d, z + d < depth)]

    def guarded(cond, run):
        if cond is None:
            run()
        else:
            pl.when(cond)(run)

    def from_column(d):
        for zz, cond in sides(d):

            def run(zz=zz):
                owner = at(zz, y, x)
                whole(owner, send_x.at[zz], to_x).wait_recv()

                @pl.when(jnp.logical_and(zz < z, has_up))
                def _():
                    upward(zz).start()

                @pl.when(jnp.logical_and(zz > z, has_down))
                def _():
                    downward(zz).start()

                start(column(zz))
                start(to_peers(owner))

            guarded(cond, run)

    def from_sides(d):
        for zz, cond in sides(d):

            def run(zz=zz):
                owner = at(zz, y, 1 - x)
                whole(owner, send_x.at[zz], to_x).wait_recv()
                part(owner, zz, 0, send_half_y.at[zz], to_y).start()
                start(to_peers(owner))
                owner = at(zz, 1 - y, x)
                whole(owner, send_x.at[zz], to_x).wait_recv()
                part(owner, zz, 1, send_half_x.at[zz], to_x).start()
                start(to_peers(owner))

            guarded(cond, run)

    def from_diagonal(d):
        for zz, cond in sides(d):

            def run(zz=zz):
                owner = at(zz, 1 - y, 1 - x)
                part(owner, zz, 0, send_half_y.at[zz], to_y).wait_recv()
                part(owner, zz, 1, send_half_x.at[zz], to_x).wait_recv()
                start(to_peers(owner))

            guarded(cond, run)

    for d in range(1, depth + 2):
        if d < depth:
            from_column(d)
        if d - 1 < depth:
            from_sides(d - 1)
        if 0 <= d - 2:
            from_diagonal(d - 2)

    def finish(zz, src=None):
        for one in column(zz, src):
            one.wait_send()
        part(at(zz, y, 1 - x), zz, 0, send_half_y.at[zz], to_y).wait_send()
        part(at(zz, 1 - y, x), zz, 1, send_half_x.at[zz], to_x).wait_send()

        @pl.when(jnp.logical_and(zz <= z, has_up))
        def _():
            upward(zz, src).wait_send()

        @pl.when(jnp.logical_and(zz >= z, has_down))
        def _():
            downward(zz, src).wait_send()

    for one in hist_copies:
        one.wait_send()
    for one in local:
        one.wait()
    for k in range(1, n_score):
        other = (c + k) % n_score
        copy(hist_ref, hist_out.at[other], hist_send.at[0], hist_recv.at[other], to_x).wait_recv()
    for zz in range(depth):
        finish(zz)
        for yy in range(2):
            for xx in range(2):
                owner = at(zz, yy, xx)

                @pl.when(owner != me)
                def _():
                    for one in to_peers(owner):
                        one.wait_send()
                    for k in range(1, n_score):
                        other = (c + k) % n_score
                        block = out_ref.at[owner, other]
                        copy(
                            block, block, send_peer.at[0, 0], recv_peer.at[owner, other], to_x
                        ).wait_recv()


def spread(cold_item_table, hist_rows):
    n_table, n_score = lax.axis_size("table"), lax.axis_size("score")
    cold_rows, width = cold_item_table.shape
    depth, rows = n_table // 4, cold_rows // n_score
    dma = pltpu.SemaphoreType.DMA
    anywhere = pl.BlockSpec(memory_space=pl.ANY)
    cold_all, hist_all = pl.pallas_call(
        functools.partial(spread_kernel, n_table, n_score),
        out_shape=(
            jax.ShapeDtypeStruct((n_table, n_score, rows, width), jnp.bfloat16),
            jax.ShapeDtypeStruct((n_score,) + hist_rows.shape, jnp.int32),
        ),
        in_specs=[pl.BlockSpec(memory_space=pltpu.VMEM)] * 2,
        out_specs=(anywhere, anywhere),
        scratch_shapes=[
            pltpu.VMEM((n_score, rows, width), jnp.bfloat16),
            dma((n_table,)),
            dma((depth, 2)),
            dma((n_table, n_score)),
            dma((depth,)),
            dma((depth,)),
            dma((depth,)),
            dma((depth,)),
            dma((depth,)),
            dma((depth,)),
            dma((n_table, n_score - 1)),
            dma((n_score - 1,)),
            dma((n_score,)),
            dma((2,)),
        ],
        compiler_params=pltpu.CompilerParams(
            collective_id=0, has_side_effects=True, vmem_limit_bytes=8 * 2**20
        ),
        name="spread_cold_rows",
    )(cold_item_table, hist_rows)
    return cold_all.reshape(n_table * cold_rows, width), hist_all


def body(
    hot_item_table, cold_item_table, hist_rows, cand_rows, w_query, w_key, w_first, w_second, w_out
):
    requests, h_dev = hist_rows.shape
    c_dev = cand_rows.shape[1]
    hot_rows, width = hot_item_table.shape
    cold_all, hist_all = spread(cold_item_table, hist_rows)
    shards = hist_all.shape[0]
    vmem = pl.BlockSpec(memory_space=pltpu.VMEM)
    smem = pl.BlockSpec(memory_space=pltpu.SMEM)
    return pl.pallas_call(
        score_kernel,
        out_shape=jax.ShapeDtypeStruct((requests, c_dev), jnp.float32),
        in_specs=[smem, smem] + [vmem] * 7,
        out_specs=vmem,
        scratch_shapes=[
            pltpu.VMEM((hot_rows + cold_all.shape[0], width), jnp.float32),
            pltpu.VMEM((requests, shards * h_dev, width), jnp.float32),
            pltpu.VMEM((requests, c_dev, width), jnp.float32),
        ],
        compiler_params=pltpu.CompilerParams(vmem_limit_bytes=56 * 2**20),
        name="score_candidates",
    )(
        hist_all,
        cand_rows,
        hot_item_table,
        cold_all,
        w_query,
        w_key,
        w_first,
        w_second[0],
        w_out,
    )


def solution(mesh):
    return jax.shard_map(
        body,
        mesh=mesh,
        in_specs=(
            P(),
            P("table", None),
            P("table", "score"),
            P("table", "score"),
            P(),
            P(),
            P(),
            P(),
            P(),
        ),
        out_specs=P("table", "score"),
        check_vma=False,
    )
```

```python
import functools
import math

import jax
import jax.numpy as jnp
from jax import lax
from jax.experimental import pallas as pl
from jax.experimental.pallas import tpu as pltpu
from jax.sharding import PartitionSpec as P

UNROLL = 32
GROUP = 2


def score_kernel(
    hist_ref,
    cand_ref,
    hot_ref,
    cold_ref,
    w_query_ref,
    w_key_ref,
    w_first_ref,
    w_second_ref,
    w_out_ref,
    out_ref,
    table,
    history,
    candidates,
):
    shards, requests, h_dev = hist_ref.shape
    c_dev = cand_ref.shape[1]
    hot_rows, width = hot_ref.shape
    h_total = shards * h_dev
    score_scale = 1.0 / math.sqrt(w_query_ref.shape[1])
    pool_scale = 1.0 / math.sqrt(h_total)

    table[pl.ds(0, hot_rows), :] = hot_ref[...]
    step = 512

    @pl.loop(0, cold_ref.shape[0] // step)
    def _(i):
        at = pl.multiple_of(i * step, step)
        to = pl.multiple_of(hot_rows + i * step, step)
        table[pl.ds(to, step), :] = cold_ref[pl.ds(at, step), :].astype(jnp.float32)

    @pl.loop(0, requests)
    def _(r):
        for s in range(shards):
            for start in range(0, h_dev, UNROLL):
                rows = [hist_ref[s, r, start + u] for u in range(UNROLL)]
                got = [table[pl.ds(row, 1), :] for row in rows]
                for u in range(UNROLL):
                    history[r, pl.ds(s * h_dev + start + u, 1), :] = got[u]
        for start in range(0, c_dev, UNROLL):
            rows = [cand_ref[r, start + u] for u in range(UNROLL)]
            got = [table[pl.ds(row, 1), :] for row in rows]
            for u in range(UNROLL):
                candidates[r, pl.ds(start + u, 1), :] = got[u]

    w_out = jnp.broadcast_to(w_out_ref[...][None, :], (16, w_out_ref.shape[0]))

    @pl.loop(0, requests // GROUP)
    def _(g):
        joined = []
        for q in range(GROUP):
            r = g * GROUP + q
            hist = history[r].astype(jnp.bfloat16)
            cand = candidates[r].astype(jnp.bfloat16)
            query = jnp.dot(cand, w_query_ref[...], preferred_element_type=jnp.float32).astype(
                jnp.bfloat16
            )
            key = jnp.dot(hist, w_key_ref[...], preferred_element_type=jnp.float32).astype(
                jnp.bfloat16
            )
            logits = lax.dot_general(
                query, key, (((1,), (1,)), ((), ())), preferred_element_type=jnp.float32
            )
            attend = (jnp.tanh(logits * (0.5 * score_scale)) * 0.5 + 0.5).astype(jnp.bfloat16)
            pooled = jnp.dot(attend, hist, preferred_element_type=jnp.float32) * pool_scale
            joined.append(jnp.concatenate([cand, pooled.astype(jnp.bfloat16)], axis=1))
        joined = jnp.concatenate(joined, axis=0)
        first = jnp.dot(joined, w_first_ref[...], preferred_element_type=jnp.float32)
        first = jnp.maximum(first, 0.0).astype(jnp.bfloat16)
        deep = jnp.dot(first, w_second_ref[...], preferred_element_type=jnp.float32)
        deep = jnp.maximum(deep, 0.0).astype(jnp.bfloat16)
        ranked = lax.dot_general(
            w_out, deep, (((1,), (1,)), ((), ())), preferred_element_type=jnp.float32
        )
        for q in range(GROUP):
            out_ref[pl.ds(g * GROUP + q, 1), :] = ranked[0:1, q * c_dev : (q + 1) * c_dev]


MESH = pl.DeviceIdType.MESH


def spread_kernel(
    n_table,
    n_score,
    cold_ref,
    hist_ref,
    out_ref,
    hist_out,
    own,
    recv_main,
    recv_diag,
    recv_peer,
    send_up,
    send_down,
    send_x,
    send_y,
    send_half_x,
    send_half_y,
    send_peer,
    hist_send,
    hist_recv,
    local_sem,
):
    depth = n_table // 4
    me = lax.axis_index("table")
    c = lax.axis_index("score")
    z, y, x = me // 4, (me // 2) % 2, me % 2
    rows = own.shape[1]
    half = rows // 2

    def at(zz, yy, xx):
        return (zz * 2 + yy) * 2 + xx

    def device(owner):
        return {"table": owner, "score": c}

    to_x, to_y = device(at(z, y, 1 - x)), device(at(z, 1 - y, x))
    to_up, to_down = device(at(z + 1, y, x)), device(at(z - 1, y, x))
    has_up, has_down = z < depth - 1, z > 0
    peers = [{"table": me, "score": (c + k) % n_score} for k in range(1, n_score)]

    barrier = pltpu.get_barrier_semaphore()
    for target in [to_x, to_y] + peers:
        pl.semaphore_signal(barrier, inc=1, device_id=target, device_id_type=MESH)
    for cond, target in ((has_up, to_up), (has_down, to_down)):

        @pl.when(cond)
        def _():
            pl.semaphore_signal(barrier, inc=1, device_id=target, device_id_type=MESH)

    for s in range(n_score):
        own[s] = cold_ref[pl.ds(s * rows, rows), :].astype(jnp.bfloat16)

    along_z = has_up.astype(jnp.int32) + has_down.astype(jnp.int32)
    pl.semaphore_wait(barrier, 2 + len(peers) + along_z)

    def copy(src, dst, send, recv, target):
        return pltpu.make_async_remote_copy(
            src_ref=src,
            dst_ref=dst,
            send_sem=send,
            recv_sem=recv,
            device_id=target,
            device_id_type=MESH,
        )

    def whole(owner, send, target, src=None):
        src = out_ref.at[owner, c] if src is None else src
        return copy(src, out_ref.at[owner, c], send, recv_main.at[owner], target)

    def part(owner, zz, which, send, target):
        block = out_ref.at[owner, c, pl.ds(which * half, half)]
        return copy(block, block, send, recv_diag.at[zz, which], target)

    def to_peers(owner):
        return [
            copy(
                out_ref.at[owner, c],
                out_ref.at[owner, c],
                send_peer.at[owner, k],
                recv_peer.at[owner, c],
                target,
            )
            for k, target in enumerate(peers)
        ]

    def start(copies):
        for one in copies:
            one.start()

    def column(zz, src=None):
        owner = at(zz, y, x)
        return [whole(owner, send_x.at[zz], to_x, src), whole(owner, send_y.at[zz], to_y, src)]

    def upward(zz, src=None):
        return whole(at(zz, y, x), send_up.at[zz], to_up, src)

    def downward(zz, src=None):
        return whole(at(zz, y, x), send_down.at[zz], to_down, src)

    mine = own.at[c]

    @pl.when(has_up)
    def _():
        upward(z, mine).start()

    @pl.when(has_down)
    def _():
        downward(z, mine).start()

    start(column(z, mine))
    hist_copies = [
        copy(hist_ref, hist_out.at[c], hist_send.at[k], hist_recv.at[c], target)
        for k, target in enumerate(peers)
    ]
    start(hist_copies)
    local = [
        pltpu.make_async_copy(own, out_ref.at[me], local_sem.at[0]),
        pltpu.make_async_copy(hist_ref, hist_out.at[c], local_sem.at[1]),
    ]
    start(local)

    def sides(d):
        if d == 0:
            return [(z, None)]
        return [(z - d, z - d >= 0), (z + d, z + d < depth)]

    def guarded(cond, run):
        if cond is None:
            run()
        else:
            pl.when(cond)(run)

    def from_column(d):
        for zz, cond in sides(d):

            def run(zz=zz):
                owner = at(zz, y, x)
                whole(owner, send_x.at[zz], to_x).wait_recv()

                @pl.when(jnp.logical_and(zz < z, has_up))
                def _():
                    upward(zz).start()

                @pl.when(jnp.logical_and(zz > z, has_down))
                def _():
                    downward(zz).start()

                start(column(zz))
                start(to_peers(owner))

            guarded(cond, run)

    def from_sides(d):
        for zz, cond in sides(d):

            def run(zz=zz):
                owner = at(zz, y, 1 - x)
                whole(owner, send_x.at[zz], to_x).wait_recv()
                part(owner, zz, 0, send_half_y.at[zz], to_y).start()
                start(to_peers(owner))
                owner = at(zz, 1 - y, x)
                whole(owner, send_x.at[zz], to_x).wait_recv()
                part(owner, zz, 1, send_half_x.at[zz], to_x).start()
                start(to_peers(owner))

            guarded(cond, run)

    def from_diagonal(d):
        for zz, cond in sides(d):

            def run(zz=zz):
                owner = at(zz, 1 - y, 1 - x)
                part(owner, zz, 0, send_half_y.at[zz], to_y).wait_recv()
                part(owner, zz, 1, send_half_x.at[zz], to_x).wait_recv()
                start(to_peers(owner))

            guarded(cond, run)

    for d in range(1, depth + 2):
        if d < depth:
            from_column(d)
        if d - 1 < depth:
            from_sides(d - 1)
        if 0 <= d - 2:
            from_diagonal(d - 2)

    def finish(zz, src=None):
        for one in column(zz, src):
            one.wait_send()
        part(at(zz, y, 1 - x), zz, 0, send_half_y.at[zz], to_y).wait_send()
        part(at(zz, 1 - y, x), zz, 1, send_half_x.at[zz], to_x).wait_send()

        @pl.when(jnp.logical_and(zz <= z, has_up))
        def _():
            upward(zz, src).wait_send()

        @pl.when(jnp.logical_and(zz >= z, has_down))
        def _():
            downward(zz, src).wait_send()

    for one in hist_copies:
        one.wait_send()
    for one in local:
        one.wait()
    for k in range(1, n_score):
        other = (c + k) % n_score
        copy(hist_ref, hist_out.at[other], hist_send.at[0], hist_recv.at[other], to_x).wait_recv()
    for zz in range(depth):
        finish(zz)
        for yy in range(2):
            for xx in range(2):
                owner = at(zz, yy, xx)

                @pl.when(owner != me)
                def _():
                    for one in to_peers(owner):
                        one.wait_send()
                    for k in range(1, n_score):
                        other = (c + k) % n_score
                        block = out_ref.at[owner, other]
                        copy(
                            block, block, send_peer.at[0, 0], recv_peer.at[owner, other], to_x
                        ).wait_recv()


def spread(cold_item_table, hist_rows):
    n_table, n_score = lax.axis_size("table"), lax.axis_size("score")
    cold_rows, width = cold_item_table.shape
    depth, rows = n_table // 4, cold_rows // n_score
    dma = pltpu.SemaphoreType.DMA
    anywhere = pl.BlockSpec(memory_space=pl.ANY)
    cold_all, hist_all = pl.pallas_call(
        functools.partial(spread_kernel, n_table, n_score),
        out_shape=(
            jax.ShapeDtypeStruct((n_table, n_score, rows, width), jnp.bfloat16),
            jax.ShapeDtypeStruct((n_score,) + hist_rows.shape, jnp.int32),
        ),
        in_specs=[pl.BlockSpec(memory_space=pltpu.VMEM)] * 2,
        out_specs=(pl.BlockSpec(memory_space=pltpu.VMEM), anywhere),
        scratch_shapes=[
            pltpu.VMEM((n_score, rows, width), jnp.bfloat16),
            dma((n_table,)),
            dma((depth, 2)),
            dma((n_table, n_score)),
            dma((depth,)),
            dma((depth,)),
            dma((depth,)),
            dma((depth,)),
            dma((depth,)),
            dma((depth,)),
            dma((n_table, n_score - 1)),
            dma((n_score - 1,)),
            dma((n_score,)),
            dma((2,)),
        ],
        compiler_params=pltpu.CompilerParams(
            collective_id=0, has_side_effects=True, vmem_limit_bytes=4 * 2**20
        ),
        name="spread_cold_rows",
    )(cold_item_table, hist_rows)
    return cold_all.reshape(n_table * cold_rows, width), hist_all


def body(
    hot_item_table, cold_item_table, hist_rows, cand_rows, w_query, w_key, w_first, w_second, w_out
):
    requests, h_dev = hist_rows.shape
    c_dev = cand_rows.shape[1]
    hot_rows, width = hot_item_table.shape
    cold_all, hist_all = spread(cold_item_table, hist_rows)
    shards = hist_all.shape[0]
    vmem = pl.BlockSpec(memory_space=pltpu.VMEM)
    smem = pl.BlockSpec(memory_space=pltpu.SMEM)
    return pl.pallas_call(
        score_kernel,
        out_shape=jax.ShapeDtypeStruct((requests, c_dev), jnp.float32),
        in_specs=[smem, smem] + [vmem] * 7,
        out_specs=vmem,
        scratch_shapes=[
            pltpu.VMEM((hot_rows + cold_all.shape[0], width), jnp.float32),
            pltpu.VMEM((requests, shards * h_dev, width), jnp.float32),
            pltpu.VMEM((requests, c_dev, width), jnp.float32),
        ],
        compiler_params=pltpu.CompilerParams(vmem_limit_bytes=36 * 2**20),
        name="score_candidates",
    )(
        hist_all,
        cand_rows,
        hot_item_table,
        cold_all,
        w_query,
        w_key,
        w_first,
        w_second[0],
        w_out,
    )


def solution(mesh):
    return jax.shard_map(
        body,
        mesh=mesh,
        in_specs=(
            P(),
            P("table", None),
            P("table", "score"),
            P("table", "score"),
            P(),
            P(),
            P(),
            P(),
            P(),
        ),
        out_specs=P("table", "score"),
        check_vma=False,
    )
```
